512 devices in a mesh: dp: 32 (over x_hi, y, core), layer: 8 (over z), query: 2 (over x_lo).
Axes of the slice: x: 4 (x_hi: 2, x_lo: 2; x = x_hi * 2 + x_lo), y: 8, z: 8, core: 2. Of those that a mesh axis runs over, the one named last changes fastest.
Arguments:
- stored_grads: bfloat16 [8192, 8, 4096], P(('dp', 'query'), 'layer'), may hold values from -6 to 6
- query_grads: bfloat16 [1024, 8, 4096], P('query', 'layer', 'dp'), may hold values from -6 to 6
- fisher_inverse: bfloat16 [8, 4096, 4096], P('layer', 'dp'), as said below
Outputs:
- influence: float32 [8192, 1024], P(('dp', 'query'))
The draws below stay inside these ranges and needn't reach their ends.
Inputs may be any that keep to these rules, and one draw needn't show every extreme that they name: fisher_inverse[l] is symmetric for every layer l, its diagonal entries lie between 0.5 and 1.6 and its other entries are under 0.03 in size.
All inputs are finite; a program needn't handle non-finite values.
Results may differ from the reference program's by a relative error of at most 0.0029.
Values may be sent and summed in bfloat16 or wider, within the bound.
No kernel may reach another device: no remote copies, remote signals or barrier semaphores. Data moves between devices by JAX's collectives and lax.ppermute only.
A program may use at most 64 MiB of HBM per device.

```python
import math
import jax
import jax.numpy as jnp
from jax import lax

F = 4096
LAYERS = 8
ROWS = 8192
QUERIES = 1024


def draw_fisher_inverse(key, part):
    key = jax.random.fold_in(key, 7)
    key_off, key_diag = jax.random.split(key)
    raw = jax.random.normal(key_off, (LAYERS, F, F), jnp.float32) * (0.31 / math.sqrt(F))
    symmetric = 0.5 * (raw + jnp.swapaxes(raw, 1, 2))
    diagonal = jnp.exp(jax.random.uniform(key_diag, (LAYERS, F), jnp.float32, math.log(0.5), math.log(1.5)))
    identity = jnp.eye(F, dtype=jnp.float32)
    return (symmetric + identity[None, :, :] * diagonal[:, :, None]).astype(jnp.bfloat16)


def shard_levels(key, dims, pieces, low, top_value):
    def one(axis_at, blocks):
        heights = jax.random.uniform(jax.random.fold_in(jax.random.fold_in(key, 6), axis_at), (blocks,), jnp.float32, low / len(pieces), top_value / len(pieces))
        return jnp.repeat(jnp.exp(heights), dims[axis_at] // blocks).reshape((-1,) + (1,) * (len(dims) - axis_at - 1))

    factor_of = one(*pieces[0])
    for cut in pieces[1:]:
        factor_of = factor_of * one(*cut)
    return factor_of


def normal_values(key, extent, scale, limit, shards=(), held_as=jnp.bfloat16):
    entries = jax.random.normal(key, extent, jnp.float32) * scale
    if len(shards) > 0:
        entries = shard_levels(key, extent, shards, -0.22, 0.18) * entries
    return jnp.clip(entries, min=-limit, max=limit).astype(held_as)


def setup_inputs(seed: int = 0) -> dict:
    arg_keys = jax.random.split(jax.random.key(seed), 4)
    return {
        "stored_grads": normal_values(arg_keys[0], (ROWS, LAYERS, F), 1.0, 6.0, ((0, 64), (1, 8))),
        "query_grads": normal_values(arg_keys[1], (QUERIES, LAYERS, F), 1.0, 6.0, ((0, 2), (1, 8), (2, 32))),
        "fisher_inverse": draw_fisher_inverse(jax.random.fold_in(arg_keys[3], 71), 0),
    }


def reference(stored_grads, query_grads, fisher_inverse):
    total = jnp.zeros((stored_grads.shape[0], query_grads.shape[0]), jnp.float32)
    for layer_index in range(LAYERS):
        precond = jnp.dot(query_grads[:, layer_index, :], fisher_inverse[layer_index], preferred_element_type=jnp.float32).astype(jnp.bfloat16)
        total = total + lax.dot_general(stored_grads[:, layer_index, :], precond, (((1,), (1,)), ((), ())), preferred_element_type=jnp.float32)
    return total * (1.0 / math.sqrt(LAYERS * F))
```

```python
import functools
import math

import jax
import jax.numpy as jnp
from jax import lax
from jax.experimental import pallas as pl
from jax.experimental.pallas import tpu as pltpu
from jax.sharding import Mesh, PartitionSpec as P

F32 = jnp.float32
BF16 = jnp.bfloat16
PARTS = 1
NT = (((1,), (1,)), ((), ()))
PARAMS = pltpu.CompilerParams(vmem_limit_bytes=40 * 1024 * 1024)
WHOLE = pl.BlockSpec(memory_space=pltpu.VMEM)
SCALARS = pl.BlockSpec(memory_space=pltpu.SMEM)


def call(body, out_shape, inputs, scratch=(), flops=0):
    size = sum(math.prod(x.shape) * x.dtype.itemsize for x in (*inputs, *out_shape))
    return pl.pallas_call(
        body,
        out_shape=[jax.ShapeDtypeStruct(s.shape, s.dtype) for s in out_shape],
        in_specs=[SCALARS if x.dtype == jnp.int32 else WHOLE for x in inputs],
        out_specs=[WHOLE] * len(out_shape),
        scratch_shapes=scratch,
        compiler_params=PARAMS,
        cost_estimate=pl.CostEstimate(flops=flops, bytes_accessed=size, transcendentals=0),
    )(*inputs)


def like(*shape, dtype=BF16):
    return jax.ShapeDtypeStruct(shape, dtype)


def pack_body(ny, w, me, x, own, other):
    for dc, out in enumerate((own, other)):
        for dx in range(2):
            for y in range(ny):
                first = (((me[0] ^ dx) * ny + y) * 2 + (me[1] ^ dc)) * w
                out[dx, :, y * w : (y + 1) * w] = x[:, pl.ds(pl.multiple_of(first, w), w)]


def pack(me, x, ny, w):
    n = x.shape[0]
    return call(functools.partial(pack_body, ny, w), [like(2, n, ny * w)] * 2, [me, x])


def fold_body(feats, f00, f01, f10, f11, own, other, held):
    ny, _, w = feats.shape
    for y in range(ny):
        held[:, y * w : (y + 1) * w] = feats[y]
    for out, blocks in ((own, (f00, f10)), (other, (f01, f11))):
        for dx in range(2):
            out[dx] = lax.dot_general(held[...], blocks[dx][...], NT, preferred_element_type=F32)


def fold(feats, blocks):
    ny, q, w = feats.shape
    return call(
        fold_body,
        [like(2, q, w, dtype=F32)] * 2,
        [feats, *blocks],
        [pltpu.VMEM((q, ny * w), BF16)],
        flops=2 * q * ny * w * 4 * w,
    )


def score_body(precond, *refs):
    blocks, (own, other, held) = refs[:-3], refs[-3:]
    ny, _, w = precond.shape
    for y in range(ny):
        held[:, y * w : (y + 1) * w] = precond[y]
    for i in range(4):
        for dc, out in enumerate((own, other)):
            out[i] = lax.dot_general(blocks[i][dc], held[...], NT, preferred_element_type=F32)


def score(precond, blocks):
    ny, q, w = precond.shape
    n = blocks[0].shape[1]
    return call(
        score_body,
        [like(4, n, q, dtype=F32)] * 2,
        [precond, *blocks],
        [pltpu.VMEM((q, ny * w), BF16)],
        flops=2 * q * ny * w * 8 * n,
    )


def meet_body(me, own, came, out):
    for x in range(2):
        for l in range(2):
            i = (x ^ me[0]) * 2 + (l ^ me[2])
            out[x * 2 + l] = (own[i] + came[i]).astype(BF16)


def meet(me, own, came):
    return call(meet_body, [like(*own.shape)], [me, own, came])[0]


def swap(x, *axes):
    sizes = [lax.axis_size(a) for a in axes]
    n = math.prod(sizes)
    return lax.ppermute(x, axes, [(i, n - 1 - i) for i in range(n)])


def spread(x, axis):
    n = lax.axis_size(axis)
    return lax.all_to_all(jnp.broadcast_to(x[None], (n,) + x.shape), axis, 0, 0, tiled=True)


def shards(stored, query, fisher):
    ny, nz, nl = lax.axis_size("y"), lax.axis_size("z"), lax.axis_size("xl")
    me = jnp.stack([lax.axis_index(a) for a in ("xh", "core", "xl")]).astype(jnp.int32)
    stored, query, fisher = stored[:, 0], query[:, 0], fisher[0]
    n, f = stored.shape
    q, w = query.shape
    qs = q // PARTS

    feats = [spread(query[h * qs : (h + 1) * qs], "y") for h in range(PARTS)]

    near, far = pack(me, fisher, ny, w)
    fish = [near[0], swap(far[0], "core"), swap(near[1], "xh"), swap(far[1], "xh", "core")]

    near, far = pack(me, stored, ny, w)
    came = swap(far, "core")
    same, cross = (jnp.stack([near[dx], came[dx]]) for dx in range(2))
    rows = [same, swap(same, "xl"), swap(cross, "xh"), swap(cross, "xh", "xl")]

    precond = []
    for h in range(PARTS):
        own, other = fold(feats[h], fish)
        both = own + swap(other, "core")
        precond.append(spread((both[0] + swap(both[1], "xh")).astype(BF16), "y"))
    scores = []
    for h in range(PARTS):
        own, other = score(precond[h], rows)
        scores.append(meet(me, own, swap(other, "core")))
    scores = scores[0] if PARTS == 1 else jnp.concatenate(scores, axis=2)
    scores = scores.reshape(2 * nl * nz, n // nz, q)
    scores = lax.all_to_all(scores, ("xh", "xl", "z"), 0, 0, tiled=True)
    scores = jnp.sum(scores.reshape(2, nl, nz, n // nz, q).astype(F32), axis=(0, 2))
    factor = 1.0 / math.sqrt(nz * f)
    total = (scores.transpose(1, 0, 2).reshape(n // nz, nl * q) * factor).astype(BF16)
    return spread(total, "z").reshape(n, nl * q).astype(F32)


def solution(mesh):
    dp, layers, queries = mesh.devices.shape
    fine = Mesh(mesh.devices.reshape(2, dp // 4, 2, layers, queries), ("xh", "y", "core", "z", "xl"))
    dp = ("xh", "y", "core")
    placed = (P((*dp, "xl"), "z", None), P("xl", "z", dp), P("z", dp, None))
    return jax.shard_map(
        shards, mesh=fine, in_specs=placed, out_specs=P((*dp, "xl"), None), check_vma=False
    )
```

```python
import functools
import math

import jax
import jax.numpy as jnp
from jax import lax
from jax.experimental import pallas as pl
from jax.experimental.pallas import tpu as pltpu
from jax.sharding import Mesh, PartitionSpec as P

F32 = jnp.float32
BF16 = jnp.bfloat16
PARTS = 2
NT = (((1,), (1,)), ((), ()))
PARAMS = pltpu.CompilerParams(vmem_limit_bytes=16 * 1024 * 1024)
WHOLE = pl.BlockSpec(memory_space=pltpu.VMEM)
ANYWHERE = pl.BlockSpec(memory_space=pl.ANY)
SCALARS = pl.BlockSpec(memory_space=pltpu.SMEM)


def call(body, out_shape, inputs, scratch=(), flops=0, after=()):
    if after:
        inner, k = body, len(after)
        body = lambda *refs: inner(*refs[k:])
    size = sum(math.prod(x.shape) * x.dtype.itemsize for x in (*inputs, *out_shape))
    return pl.pallas_call(
        body,
        out_shape=[jax.ShapeDtypeStruct(s.shape, s.dtype) for s in out_shape],
        in_specs=[ANYWHERE] * len(after) + [SCALARS if x.dtype == jnp.int32 else WHOLE for x in inputs],
        out_specs=[WHOLE] * len(out_shape),
        scratch_shapes=scratch,
        compiler_params=PARAMS,
        cost_estimate=pl.CostEstimate(flops=flops, bytes_accessed=size, transcendentals=0),
    )(*after, *inputs)


def like(*shape, dtype=BF16):
    return jax.ShapeDtypeStruct(shape, dtype)


def pack_body(ny, w, me, fisher, stored, f00, f01, f10, f11, own, other):
    for x, outs in ((fisher, ((f00, f10), (f01, f11))), (stored, ([own.at[0], own.at[1]], [other.at[0], other.at[1]]))):
        for dc in range(2):
            for dx in range(2):
                for y in range(ny):
                    first = (((me[0] ^ dx) * ny + y) * 2 + (me[1] ^ dc)) * w
                    outs[dc][dx][:, y * w : (y + 1) * w] = x[:, pl.ds(pl.multiple_of(first, w), w)]


def pack(me, fisher, stored, ny, w):
    n, g = stored.shape[0], fisher.shape[0]
    shapes = [like(g, ny * w)] * 4 + [like(2, n, ny * w)] * 2
    return call(functools.partial(pack_body, ny, w), shapes, [me, fisher, stored])


def pair_body(near, came, same, cross):
    for dx, out in enumerate((same, cross)):
        out[0], out[1] = near[dx], came[dx]


def pair(near, came):
    return call(pair_body, [like(*near.shape)] * 2, [near, came])


def copies_body(x, out):
    for i in range(out.shape[0]):
        out[i] = x[...]


def copies(x, n, after=()):
    return call(copies_body, [like(n, *x.shape)], [x], after=after)[0]


def settle_body(own, came, last, out):
    done = (own[...] + came[0] + last[...]).astype(BF16)
    for i in range(out.shape[0]):
        out[i] = done


def settle(own, came, last, n, after=()):
    return call(settle_body, [like(n, *own.shape)], [own, came, last], after=after)[0]


def fold_body(feats, f00, f01, f10, f11, own, own_x, other, held):
    ny, _, w = feats.shape
    for y in range(ny):
        held[:, y * w : (y + 1) * w] = feats[y]

    def dot(block):
        return lax.dot_general(held[...], block[...], NT, preferred_element_type=F32)

    other[0], other[1] = dot(f01), dot(f11)
    own[...], own_x[...] = dot(f00), dot(f10)


def fold(feats, blocks, after=()):
    ny, q, w = feats.shape
    return call(
        fold_body,
        [like(q, w, dtype=F32), like(q, w, dtype=F32), like(2, q, w, dtype=F32)],
        [feats, *blocks],
        [pltpu.VMEM((q, ny * w), BF16)],
        flops=2 * q * ny * w * 4 * w,
        after=after,
    )


def score_body(precond, *refs):
    blocks, (own, other, held) = refs[:-3], refs[-3:]
    ny, _, w = precond.shape
    for y in range(ny):
        held[:, y * w : (y + 1) * w] = precond[y]
    for i in range(4):
        for dc, out in enumerate((own, other)):
            out[i] = lax.dot_general(blocks[i][dc], held[...], NT, preferred_element_type=F32)


def score(precond, blocks):
    ny, q, w = precond.shape
    n = blocks[0].shape[1]
    return call(
        score_body,
        [like(4, n, q, dtype=F32)] * 2,
        [precond, *blocks],
        [pltpu.VMEM((q, ny * w), BF16)],
        flops=2 * q * ny * w * 8 * n,
    )


def meet_body(me, *refs):
    terms, out = refs[:-1], refs[-1]
    for h in range(len(terms) // 2):
        own, came = terms[2 * h : 2 * h + 2]
        q = own.shape[2]
        for x in range(2):
            for l in range(2):
                i = (x ^ me[0]) * 2 + (l ^ me[2])
                out[x * 2 + l, :, h * q : (h + 1) * q] = (own[i] + came[i]).astype(BF16)


def meet(me, terms):
    k, n, q = terms[0].shape
    return call(meet_body, [like(k, n, q * (len(terms) // 2))], [me, *terms])[0]


def finish_body(factor, scores, out):
    nx, nl, nz, rows, q = scores.shape
    for l in range(nl):
        total = jnp.zeros((rows, q), F32)
        for x in range(nx):
            for z in range(nz):
                total += scores[x, l, z].astype(F32)
        total = (total * factor).astype(BF16)
        for z in range(nz):
            out[z, :, l * q : (l + 1) * q] = total


def finish(scores, factor):
    _, nl, nz, rows, q = scores.shape
    return call(functools.partial(finish_body, factor), [like(nz, rows, nl * q)], [scores])[0]


def swap(x, *axes):
    sizes = [lax.axis_size(a) for a in axes]
    n = math.prod(sizes)
    return lax.ppermute(x, axes, [(i, n - 1 - i) for i in range(n)])


def trade(x, *axes):
    return lax.all_to_all(x, axes, 0, 0, tiled=True)


def shards(stored, query, fisher):
    ny, nz, nl = lax.axis_size("y"), lax.axis_size("z"), lax.axis_size("xl")
    me = jnp.stack([lax.axis_index(a) for a in ("xh", "core", "xl")]).astype(jnp.int32)
    stored, query, fisher = stored[:, 0], query[:, 0], fisher[0]
    n, f = stored.shape
    q, w = query.shape

    f00, f01, f10, f11, near, far = pack(me, fisher, stored, ny, w)
    fish = [f00, swap(f01, "core"), swap(f10, "xh"), swap(f11, "xh", "core")]
    same, cross = pair(near, swap(far, "core"))
    rows = [same, swap(same, "xl"), swap(cross, "xh"), swap(cross, "xh", "xl")]

    before_gather = ((), fish[1:])
    before_fold = ((same,), (rows[1],))
    before_settle = ((), (rows[2], rows[3]))
    half = q // PARTS
    feats = [
        trade(copies(query[h * half : (h + 1) * half], ny, before_gather[h]), "y") for h in range(PARTS)
    ]
    precond = []
    for h in range(PARTS):
        own, own_x, other = fold(feats[h], fish, before_fold[h])
        came = swap(other, "core")
        full = settle(own, came, swap(own_x + came[1], "xh"), ny, before_settle[h])
        precond.append(trade(full, "y"))
    terms = []
    for h in range(PARTS):
        own, other = score(precond[h], rows)
        terms += [own, swap(other, "core")]
    scores = trade(meet(me, terms).reshape(2 * nl * nz, n // nz, q), "xh", "xl", "z")
    total = finish(scores.reshape(2, nl, nz, n // nz, q), 1.0 / math.sqrt(nz * f))
    return trade(total, "z").reshape(n, nl * q).astype(F32)


def solution(mesh):
    dp, layers, queries = mesh.devices.shape
    fine = Mesh(mesh.devices.reshape(2, dp // 4, 2, layers, queries), ("xh", "y", "core", "z", "xl"))
    dp = ("xh", "y", "core")
    placed = (P((*dp, "xl"), "z", None), P("xl", "z", dp), P("z", dp, None))
    return jax.shard_map(
        shards, mesh=fine, in_specs=placed, out_specs=P((*dp, "xl"), None), check_vma=False
    )
```

```python
import functools
import math

import jax
import jax.numpy as jnp
from jax import lax
from jax.experimental import pallas as pl
from jax.experimental.pallas import tpu as pltpu
from jax.sharding import Mesh, PartitionSpec as P

F32 = jnp.float32
BF16 = jnp.bfloat16
NT = (((1,), (1,)), ((), ()))
PARAMS = pltpu.CompilerParams(vmem_limit_bytes=40 * 1024 * 1024)
WHOLE = pl.BlockSpec(memory_space=pltpu.VMEM)
ANYWHERE = pl.BlockSpec(memory_space=pl.ANY)
SCALARS = pl.BlockSpec(memory_space=pltpu.SMEM)


def call(body, out_shape, inputs, scratch=(), flops=0, after=()):
    if after:
        inner, k = body, len(after)
        body = lambda *refs: inner(*refs[k:])
    size = sum(math.prod(x.shape) * x.dtype.itemsize for x in (*inputs, *out_shape))
    return pl.pallas_call(
        body,
        out_shape=[jax.ShapeDtypeStruct(s.shape, s.dtype) for s in out_shape],
        in_specs=[ANYWHERE] * len(after) + [SCALARS if x.dtype == jnp.int32 else WHOLE for x in inputs],
        out_specs=[WHOLE] * len(out_shape),
        scratch_shapes=scratch,
        compiler_params=PARAMS,
        cost_estimate=pl.CostEstimate(flops=flops, bytes_accessed=size, transcendentals=0),
    )(*after, *inputs)


def like(*shape, dtype=BF16):
    return jax.ShapeDtypeStruct(shape, dtype)


def pack_body(ny, w, me, fisher, stored, f00, f01, f10, f11, own, other):
    for x, outs in ((fisher, ((f00, f10), (f01, f11))), (stored, ([own.at[0], own.at[1]], [other.at[0], other.at[1]]))):
        for dc in range(2):
            for dx in range(2):
                for y in range(ny):
                    first = (((me[0] ^ dx) * ny + y) * 2 + (me[1] ^ dc)) * w
                    outs[dc][dx][:, y * w : (y + 1) * w] = x[:, pl.ds(pl.multiple_of(first, w), w)]


def pack(me, fisher, stored, ny, w):
    n, g = stored.shape[0], fisher.shape[0]
    shapes = [like(g, ny * w)] * 4 + [like(2, n, ny * w)] * 2
    return call(functools.partial(pack_body, ny, w), shapes, [me, fisher, stored])


def pair_body(near, came, same, cross):
    for dx, out in enumerate((same, cross)):
        out[0], out[1] = near[dx], came[dx]


def pair(near, came):
    return call(pair_body, [like(*near.shape)] * 2, [near, came])


def copies_body(x, out):
    for i in range(out.shape[0]):
        out[i] = x[...]


def copies(x, n):
    return call(copies_body, [like(n, *x.shape)], [x])[0]


def settle_body(own, came, last, out):
    done = (own[...] + came[0] + last[...]).astype(BF16)
    for i in range(out.shape[0]):
        out[i] = done


def settle(own, came, last, n):
    return call(settle_body, [like(n, *own.shape)], [own, came, last])[0]


def join(held, parts):
    ny, _, w = parts.shape
    for y in range(ny):
        held[:, y * w : (y + 1) * w] = parts[y]


def fold_body(feats, f0, f1, out, out_x, held):
    join(held, feats)
    out_x[...] = lax.dot_general(held[...], f1[...], NT, preferred_element_type=F32)
    out[...] = lax.dot_general(held[...], f0[...], NT, preferred_element_type=F32)


def fold(feats, blocks, after=()):
    ny, q, w = feats.shape
    return call(
        fold_body,
        [like(q, w, dtype=F32)] * 2,
        [feats, *blocks],
        [pltpu.VMEM((q, ny * w), BF16)],
        flops=2 * q * ny * w * 2 * w,
        after=after,
    )


def fold_far_body(feats, f0, f1, out, held):
    fold_body(feats, f0, f1, out.at[0], out.at[1], held)


def fold_far(feats, blocks, after=()):
    ny, q, w = feats.shape
    return call(
        fold_far_body,
        [like(2, q, w, dtype=F32)],
        [feats, *blocks],
        [pltpu.VMEM((q, ny * w), BF16)],
        flops=2 * q * ny * w * 2 * w,
        after=after,
    )[0]


def score_body(dc, precond, b0, b1, b2, b3, out, held):
    join(held, precond)
    for i, block in enumerate((b0, b1, b2, b3)):
        out[i] = lax.dot_general(block[dc], held[...], NT, preferred_element_type=F32)


def score(dc, precond, blocks):
    ny, q, w = precond.shape
    n = blocks[0].shape[1]
    return call(
        functools.partial(score_body, dc),
        [like(4, n, q, dtype=F32)],
        [precond, *blocks],
        [pltpu.VMEM((q, ny * w), BF16)],
        flops=2 * q * ny * w * 4 * n,
    )[0]


def meet_body(me, *refs):
    terms, out = refs[:-1], refs[-1]
    for h in range(len(terms) // 2):
        own, came = terms[2 * h : 2 * h + 2]
        q = own.shape[2]
        for x in range(2):
            for l in range(2):
                i = (x ^ me[0]) * 2 + (l ^ me[2])
                out[x * 2 + l, :, h * q : (h + 1) * q] = (own[i] + came[i]).astype(BF16)


def meet(me, terms):
    k, n, q = terms[0].shape
    return call(meet_body, [like(k, n, q * (len(terms) // 2))], [me, *terms])[0]


def finish_body(factor, scores, out):
    nx, nl, nz, rows, q = scores.shape
    for l in range(nl):
        total = jnp.zeros((rows, q), F32)
        for x in range(nx):
            for z in range(nz):
                total += scores[x, l, z].astype(F32)
        total = (total * factor).astype(BF16)
        for z in range(nz):
            out[z, :, l * q : (l + 1) * q] = total


def finish(scores, factor):
    _, nl, nz, rows, q = scores.shape
    return call(functools.partial(finish_body, factor), [like(nz, rows, nl * q)], [scores])[0]


def swap(x, *axes):
    sizes = [lax.axis_size(a) for a in axes]
    n = math.prod(sizes)
    return lax.ppermute(x, axes, [(i, n - 1 - i) for i in range(n)])


def trade(x, *axes):
    return lax.all_to_all(x, axes, 0, 0, tiled=True)


def shards(stored, query, fisher):
    ny, nz, nl = lax.axis_size("y"), lax.axis_size("z"), lax.axis_size("xl")
    me = jnp.stack([lax.axis_index(a) for a in ("xh", "core", "xl")]).astype(jnp.int32)
    stored, query, fisher = stored[:, 0], query[:, 0], fisher[0]
    n, f = stored.shape
    q, w = query.shape

    f00, f01, f10, f11, near, far = pack(me, fisher, stored, ny, w)
    fish = (f00, swap(f10, "xh")), (swap(f01, "core"), swap(f11, "xh", "core"))
    same, cross = pair(near, swap(far, "core"))
    rows = [same, swap(same, "xl"), swap(cross, "xh"), swap(cross, "xh", "xl")]

    feats = trade(copies(query, ny), "y")
    came = swap(fold_far(feats, fish[1], (same, fish[0][1])), "core")
    own, own_x = fold(feats, fish[0])
    precond = trade(settle(own, came, swap(own_x + came[1], "xh"), ny), "y")
    came = swap(score(1, precond, rows), "core")
    terms = [score(0, precond, rows), came]
    scores = trade(meet(me, terms).reshape(2 * nl * nz, n // nz, q), "xh", "xl", "z")
    total = finish(scores.reshape(2, nl, nz, n // nz, q), 1.0 / math.sqrt(nz * f))
    return trade(total, "z").reshape(n, nl * q).astype(F32)


def solution(mesh):
    dp, layers, queries = mesh.devices.shape
    fine = Mesh(mesh.devices.reshape(2, dp // 4, 2, layers, queries), ("xh", "y", "core", "z", "xl"))
    dp = ("xh", "y", "core")
    placed = (P((*dp, "xl"), "z", None), P("xl", "z", dp), P("z", dp, None))
    return jax.shard_map(
        shards, mesh=fine, in_specs=placed, out_specs=P((*dp, "xl"), None), check_vma=False
    )
```

```python
import functools
import math

import jax
import jax.numpy as jnp
from jax import lax
from jax.experimental import pallas as pl
from jax.experimental.pallas import tpu as pltpu
from jax.sharding import Mesh, PartitionSpec as P

F32 = jnp.float32
BF16 = jnp.bfloat16
NT = (((1,), (1,)), ((), ()))
PARAMS = pltpu.CompilerParams(vmem_limit_bytes=40 * 1024 * 1024)
WHOLE = pl.BlockSpec(memory_space=pltpu.VMEM)
ANYWHERE = pl.BlockSpec(memory_space=pl.ANY)
SCALARS = pl.BlockSpec(memory_space=pltpu.SMEM)


def call(body, out_shape, inputs, scratch=(), flops=0, after=()):
    if after:
        inner, k = body, len(after)
        body = lambda *refs: inner(*refs[k:])
    size = sum(math.prod(x.shape) * x.dtype.itemsize for x in (*inputs, *out_shape))
    return pl.pallas_call(
        body,
        out_shape=[jax.ShapeDtypeStruct(s.shape, s.dtype) for s in out_shape],
        in_specs=[ANYWHERE] * len(after) + [SCALARS if x.dtype == jnp.int32 else WHOLE for x in inputs],
        out_specs=[WHOLE] * len(out_shape),
        scratch_shapes=scratch,
        compiler_params=PARAMS,
        cost_estimate=pl.CostEstimate(flops=flops, bytes_accessed=size, transcendentals=0),
    )(*after, *inputs)


def like(*shape, dtype=BF16):
    return jax.ShapeDtypeStruct(shape, dtype)


def pack_body(ny, w, me, fisher, stored, f_near, f_far, f_cross, s_same, s_cross):
    for x, outs in ((fisher, ((f_near, f_far), f_cross)), (stored, (s_same, s_cross))):
        for dx in range(2):
            for dc in range(2):
                out = outs[dx][dc] if isinstance(outs[dx], tuple) else outs[dx].at[dc]
                for y in range(ny):
                    first = (((me[0] ^ dx) * ny + y) * 2 + (me[1] ^ dc)) * w
                    out[:, y * w : (y + 1) * w] = x[:, pl.ds(pl.multiple_of(first, w), w)]


def pack(me, fisher, stored, ny, w):
    n, g = stored.shape[0], fisher.shape[0]
    shapes = [like(g, ny * w)] * 2 + [like(2, g, ny * w)] + [like(2, n, ny * w)] * 2
    return call(functools.partial(pack_body, ny, w), shapes, [me, fisher, stored])


def gather_far_body(*refs):
    blocks, out = refs[:-1], refs[-1]
    for i, block in enumerate(blocks):
        out[i] = block[...] if len(block.shape) == 2 else block[1]


def gather_far(blocks):
    return call(gather_far_body, [like(len(blocks), *blocks[0].shape[-2:])], blocks)[0]


def copies_body(x, out):
    for i in range(out.shape[0]):
        out[i] = x[...]


def copies(x, n):
    return call(copies_body, [like(n, *x.shape)], [x])[0]


def settle_body(own, came, last, out):
    done = (own[...] + came[0] + last[...]).astype(BF16)
    for i in range(out.shape[0]):
        out[i] = done


def settle(own, came, last, n):
    return call(settle_body, [like(n, *own.shape)], [own, came, last])[0]


def join(held, parts):
    ny, _, w = parts.shape
    for y in range(ny):
        held[:, y * w : (y + 1) * w] = parts[y]


def join(held, parts):
    ny, _, w = parts.shape
    for y in range(ny):
        held[:, y * w : (y + 1) * w] = parts[y]


def fold_body(feats, near, cross, out, out_x, held):
    join(held, feats)
    out_x[...] = lax.dot_general(held[...], cross[0], NT, preferred_element_type=F32)
    out[...] = lax.dot_general(held[...], near[...], NT, preferred_element_type=F32)


def fold(feats, near, cross):
    ny, q, w = feats.shape
    return call(
        fold_body,
        [like(q, w, dtype=F32)] * 2,
        [feats, near, cross],
        [pltpu.VMEM((q, ny * w), BF16)],
        flops=2 * q * ny * w * 2 * w,
    )


def fold_far_body(feats, blocks, out, held):
    join(held, feats)
    for dx in range(2):
        out[dx] = lax.dot_general(held[...], blocks[dx], NT, preferred_element_type=F32)


def fold_far(feats, blocks, after=()):
    ny, q, w = feats.shape
    return call(
        fold_far_body,
        [like(2, q, w, dtype=F32)],
        [feats, blocks],
        [pltpu.VMEM((q, ny * w), BF16)],
        flops=2 * q * ny * w * 2 * w,
        after=after,
    )[0]


def score_body(precond, *refs):
    blocks, (out, held) = refs[:-2], refs[-2:]
    join(held, precond)
    i = 0
    for block in blocks:
        for k in range(block.shape[0] if len(blocks) == 2 else 1):
            out[i] = lax.dot_general(block[k], held[...], NT, preferred_element_type=F32)
            i += 1


def score(precond, blocks):
    ny, q, w = precond.shape
    n = blocks[0].shape[1]
    return call(
        score_body,
        [like(4, n, q, dtype=F32)],
        [precond, *blocks],
        [pltpu.VMEM((q, ny * w), BF16)],
        flops=2 * q * ny * w * 4 * n,
    )[0]


def meet_body(me, *refs):
    terms, out = refs[:-1], refs[-1]
    for h in range(len(terms) // 2):
        own, came = terms[2 * h : 2 * h + 2]
        q = own.shape[2]
        for x in range(2):
            for l in range(2):
                i = (x ^ me[0]) * 2 + ((x ^ me[0]) ^ (l ^ me[2]))
                out[x * 2 + l, :, h * q : (h + 1) * q] = (own[i] + came[i]).astype(BF16)


def meet(me, terms):
    k, n, q = terms[0].shape
    return call(meet_body, [like(k, n, q * (len(terms) // 2))], [me, *terms])[0]


def finish_body(factor, scores, out):
    nx, nl, nz, rows, q = scores.shape
    for l in range(nl):
        total = jnp.zeros((rows, q), F32)
        for x in range(nx):
            for z in range(nz):
                total += scores[x, l, z].astype(F32)
        total = (total * factor).astype(BF16)
        for z in range(nz):
            out[z, :, l * q : (l + 1) * q] = total


def finish(scores, factor):
    _, nl, nz, rows, q = scores.shape
    return call(functools.partial(finish_body, factor), [like(nz, rows, nl * q)], [scores])[0]


def swap(x, *axes):
    sizes = [lax.axis_size(a) for a in axes]
    n = math.prod(sizes)
    return lax.ppermute(x, axes, [(i, n - 1 - i) for i in range(n)])


def trade(x, *axes):
    return lax.all_to_all(x, axes, 0, 0, tiled=True)


def shards(stored, query, fisher):
    ny, nz, nl = lax.axis_size("y"), lax.axis_size("z"), lax.axis_size("xl")
    me = jnp.stack([lax.axis_index(a) for a in ("xh", "core", "xl")]).astype(jnp.int32)
    stored, query, fisher = stored[:, 0], query[:, 0], fisher[0]
    n, f = stored.shape
    q, w = query.shape

    f_near, f_far, f_cross, s_same, s_cross = pack(me, fisher, stored, ny, w)
    f_cross = swap(f_cross, "xh", "xl")
    f_far = swap(gather_far([f_far, f_cross]), "core")
    s_side = swap(s_same, "xl")
    s_across = swap(s_cross, "xh", "xl")
    s_passed = swap(s_across, "xl")

    feats = trade(copies(query, ny), "y")
    came = swap(fold_far(feats, f_far, (s_side, s_across)), "core")
    own, own_x = fold(feats, f_near, f_cross)
    precond = trade(settle(own, came, swap(own_x + came[1], "xh"), ny), "y")
    far = [swap(gather_far([s_same, s_side, s_across]), "core"), swap(gather_far([s_passed]), "core")]
    came = swap(score(precond, far), "core")
    terms = [score(precond, [s_same, s_side, s_across, s_passed]), came]
    scores = trade(meet(me, terms).reshape(2 * nl * nz, n // nz, q), "xh", "xl", "z")
    total = finish(scores.reshape(2, nl, nz, n // nz, q), 1.0 / math.sqrt(nz * f))
    return trade(total, "z").reshape(n, nl * q).astype(F32)


def solution(mesh):
    dp, layers, queries = mesh.devices.shape
    fine = Mesh(mesh.devices.reshape(2, dp // 4, 2, layers, queries), ("xh", "y", "core", "z", "xl"))
    dp = ("xh", "y", "core")
    placed = (P((*dp, "xl"), "z", None), P("xl", "z", dp), P("z", dp, None))
    return jax.shard_map(
        shards, mesh=fine, in_specs=placed, out_specs=P((*dp, "xl"), None), check_vma=False
    )
```

```python
import functools
import math

import jax
import jax.numpy as jnp
from jax import lax
from jax.experimental import pallas as pl
from jax.experimental.pallas import tpu as pltpu
from jax.sharding import Mesh, PartitionSpec as P

F32 = jnp.float32
BF16 = jnp.bfloat16
NT = (((1,), (1,)), ((), ()))
PARAMS = pltpu.CompilerParams(vmem_limit_bytes=40 * 1024 * 1024)
WHOLE = pl.BlockSpec(memory_space=pltpu.VMEM)
ANYWHERE = pl.BlockSpec(memory_space=pl.ANY)
SCALARS = pl.BlockSpec(memory_space=pltpu.SMEM)


def call(body, out_shape, inputs, scratch=(), flops=0, after=()):
    if after:
        inner, k = body, len(after)
        body = lambda *refs: inner(*refs[k:])
    size = sum(math.prod(x.shape) * x.dtype.itemsize for x in (*inputs, *out_shape))
    return pl.pallas_call(
        body,
        out_shape=[jax.ShapeDtypeStruct(s.shape, s.dtype) for s in out_shape],
        in_specs=[ANYWHERE] * len(after) + [SCALARS if x.dtype == jnp.int32 else WHOLE for x in inputs],
        out_specs=[WHOLE] * len(out_shape),
        scratch_shapes=scratch,
        compiler_params=PARAMS,
        cost_estimate=pl.CostEstimate(flops=flops, bytes_accessed=size, transcendentals=0),
    )(*after, *inputs)


def like(*shape, dtype=BF16):
    return jax.ShapeDtypeStruct(shape, dtype)


def pack_body(ny, w, me, fisher, stored, f00, f01, f10, f11, near0, near1, far):
    for x, outs in ((fisher, ((f00, f10), (f01, f11))), (stored, ((near0, near1), (far.at[0], far.at[1])))):
        for dc in range(2):
            for dx in range(2):
                for y in range(ny):
                    first = (((me[0] ^ dx) * ny + y) * 2 + (me[1] ^ dc)) * w
                    outs[dc][dx][:, y * w : (y + 1) * w] = x[:, pl.ds(pl.multiple_of(first, w), w)]


def pack(me, fisher, stored, ny, w):
    n, g = stored.shape[0], fisher.shape[0]
    shapes = [like(g, ny * w)] * 4 + [like(n, ny * w)] * 2 + [like(2, n, ny * w)]
    return call(functools.partial(pack_body, ny, w), shapes, [me, fisher, stored])


def part_body(near1, came, cross):
    cross[0], cross[1] = near1[...], came[1]


def part(near1, came):
    return call(part_body, [like(*came.shape)], [near1, came])[0]


def copies_body(x, out, block, came, sems):
    load = pltpu.make_async_copy(x, block, came)
    load.start()
    load.wait()
    moves = [pltpu.make_async_copy(block, out.at[i], sems.at[i]) for i in range(out.shape[0])]
    for move in moves:
        move.start()
    for move in moves:
        move.wait()


def copies(x, n):
    return pl.pallas_call(
        copies_body,
        out_shape=like(n, *x.shape),
        in_specs=[ANYWHERE],
        out_specs=ANYWHERE,
        scratch_shapes=[pltpu.VMEM(x.shape, BF16), pltpu.SemaphoreType.DMA, pltpu.SemaphoreType.DMA((n,))],
    )(x)


def settle_body(own, came, last, out):
    done = (own[...] + came[0] + last[...]).astype(BF16)
    for i in range(out.shape[0]):
        out[i] = done


def settle(own, came, last, n):
    return call(settle_body, [like(n, *own.shape)], [own, came, last])[0]


def join(held, parts):
    ny, _, w = parts.shape
    for y in range(ny):
        held[:, y * w : (y + 1) * w] = parts[y]


def fold_body(feats, f0, f1, out, out_x, held):
    join(held, feats)
    out_x[...] = lax.dot_general(held[...], f1[...], NT, preferred_element_type=F32)
    out[...] = lax.dot_general(held[...], f0[...], NT, preferred_element_type=F32)


def fold(feats, blocks, after=()):
    ny, q, w = feats.shape
    return call(
        fold_body,
        [like(q, w, dtype=F32)] * 2,
        [feats, *blocks],
        [pltpu.VMEM((q, ny * w), BF16)],
        flops=2 * q * ny * w * 2 * w,
        after=after,
    )


def fold_far_body(feats, f0, f1, out, held):
    fold_body(feats, f0, f1, out.at[0], out.at[1], held)


def fold_far(feats, blocks, after=()):
    ny, q, w = feats.shape
    return call(
        fold_far_body,
        [like(2, q, w, dtype=F32)],
        [feats, *blocks],
        [pltpu.VMEM((q, ny * w), BF16)],
        flops=2 * q * ny * w * 2 * w,
        after=after,
    )[0]


def score_body(dc, same, side, precond, cross, twin, out, held, rows, sems):
    loads = [
        pltpu.make_async_copy(block if len(block.shape) == 2 else block.at[0], rows.at[i], sems.at[i])
        for i, block in enumerate((same, side))
    ]
    for load in loads:
        load.start()
    join(held, precond)
    for i, block in ((2, cross), (3, twin)):
        out[i] = lax.dot_general(block[dc], held[...], NT, preferred_element_type=F32)
    for i, load in enumerate(loads):
        load.wait()
        out[i] = lax.dot_general(rows[i], held[...], NT, preferred_element_type=F32)


def score(dc, precond, same, side, cross, twin):
    ny, q, w = precond.shape
    n, k = side.shape
    return pl.pallas_call(
        functools.partial(score_body, dc),
        out_shape=like(4, n, q, dtype=F32),
        in_specs=[pl.BlockSpec(memory_space=pltpu.HBM)] * 2 + [WHOLE] * 3,
        out_specs=WHOLE,
        scratch_shapes=[pltpu.VMEM((q, k), BF16), pltpu.VMEM((2, n, k), BF16), pltpu.SemaphoreType.DMA((2,))],
        compiler_params=PARAMS,
        cost_estimate=pl.CostEstimate(flops=2 * q * k * 4 * n, bytes_accessed=4 * 1024 * 1024, transcendentals=0),
    )(
        pltpu.with_memory_space_constraint(same, pltpu.HBM),
        pltpu.with_memory_space_constraint(side, pltpu.HBM),
        precond,
        cross,
        twin,
    )


def meet_body(me, own, came, out):
    nz, _, rows, _ = out.shape
    for x in range(2):
        for l in range(2):
            i = (x ^ me[0]) * 2 + (l ^ me[2])
            total = (own[i] + came[i]).astype(BF16)
            for z in range(nz):
                out[z, x * 2 + l] = total[z * rows : (z + 1) * rows]


def meet(me, own, came, nz):
    k, n, q = own.shape
    return call(meet_body, [like(nz, k, n // nz, q)], [me, own, came])[0]


def finish_body(factor, scores, out):
    nz, nx, nl, rows, q = scores.shape
    for l in range(nl):
        total = jnp.zeros((rows, q), F32)
        for x in range(nx):
            for z in range(nz):
                total += scores[z, x, l].astype(F32)
        total = (total * factor).astype(BF16)
        for z in range(nz):
            out[z, :, l * q : (l + 1) * q] = total


def finish(scores, factor):
    nz, _, nl, rows, q = scores.shape
    return call(functools.partial(finish_body, factor), [like(nz, rows, nl * q)], [scores])[0]


def swap(x, *axes):
    sizes = [lax.axis_size(a) for a in axes]
    n = math.prod(sizes)
    return lax.ppermute(x, axes, [(i, n - 1 - i) for i in range(n)])


def trade(x, *axes):
    return lax.all_to_all(x, axes, 0, 0, tiled=True)


def shards(stored, query, fisher):
    ny, nz, nl = lax.axis_size("y"), lax.axis_size("z"), lax.axis_size("xl")
    me = jnp.stack([lax.axis_index(a) for a in ("xh", "core", "xl")]).astype(jnp.int32)
    stored, query, fisher = stored[:, 0], query[:, 0], fisher[0]
    n, f = stored.shape
    q, w = query.shape

    f00, f01, f10, f11, near0, near1, far = pack(me, fisher, stored, ny, w)
    fish = (f00, swap(f10, "xh", "xl")), (swap(f01, "core"), swap(f11, "xh", "core", "xl"))
    came = swap(far, "core")
    cross = part(near1, came)
    side = swap(near0, "xl")

    feats = trade(copies(query, ny), "y")
    total = swap(fold_far(feats, fish[1], (cross, fish[0][1], side)), "core")
    own, own_x = fold(feats, fish[0])
    precond = trade(settle(own, total, swap(own_x + total[1], "xh"), ny), "y")
    twin, cross = swap(cross, "xh", "xl"), swap(cross, "xh")
    far = swap(score(1, precond, came, swap(came[0], "xl"), cross, twin), "core")
    terms = [score(0, precond, near0, side, cross, twin), far]
    scores = trade(meet(me, *terms, nz).reshape(nz * 2 * nl, n // nz, q), "z", "xh", "xl")
    total = finish(scores.reshape(nz, 2, nl, n // nz, q), 1.0 / math.sqrt(nz * f))
    return trade(total, "z").reshape(n, nl * q).astype(F32)


def solution(mesh):
    dp, layers, queries = mesh.devices.shape
    fine = Mesh(mesh.devices.reshape(2, dp // 4, 2, layers, queries), ("xh", "y", "core", "z", "xl"))
    dp = ("xh", "y", "core")
    placed = (P((*dp, "xl"), "z", None), P("xl", "z", dp), P("z", dp, None))
    return jax.shard_map(
        shards, mesh=fine, in_specs=placed, out_specs=P((*dp, "xl"), None), check_vma=False
    )
```

```python
import functools
import math

import jax
import jax.numpy as jnp
from jax import lax
from jax.experimental import pallas as pl
from jax.experimental.pallas import tpu as pltpu
from jax.sharding import Mesh, PartitionSpec as P

F32 = jnp.float32
BF16 = jnp.bfloat16
NT = (((1,), (1,)), ((), ()))
PARAMS = pltpu.CompilerParams(vmem_limit_bytes=40 * 1024 * 1024)
WHOLE = pl.BlockSpec(memory_space=pltpu.VMEM)
ANYWHERE = pl.BlockSpec(memory_space=pl.ANY)
SCALARS = pl.BlockSpec(memory_space=pltpu.SMEM)


def call(body, out_shape, inputs, scratch=(), flops=0, after=()):
    if after:
        inner, k = body, len(after)
        body = lambda *refs: inner(*refs[k:])
    size = sum(math.prod(x.shape) * x.dtype.itemsize for x in (*inputs, *out_shape))
    return pl.pallas_call(
        body,
        out_shape=[jax.ShapeDtypeStruct(s.shape, s.dtype) for s in out_shape],
        in_specs=[ANYWHERE] * len(after) + [SCALARS if x.dtype == jnp.int32 else WHOLE for x in inputs],
        out_specs=[WHOLE] * len(out_shape),
        scratch_shapes=scratch,
        compiler_params=PARAMS,
        cost_estimate=pl.CostEstimate(flops=flops, bytes_accessed=size, transcendentals=0),
    )(*after, *inputs)


def like(*shape, dtype=BF16):
    return jax.ShapeDtypeStruct(shape, dtype)


def pack_body(ny, w, me, fisher, stored, f00, f01, f10, f11, near0, near1, far):
    for x, outs in ((fisher, ((f00, f10), (f01, f11))), (stored, ((near0, near1), (far.at[0], far.at[1])))):
        for dc in range(2):
            for dx in range(2):
                for y in range(ny):
                    first = (((me[0] ^ dx) * ny + y) * 2 + (me[1] ^ dc)) * w
                    outs[dc][dx][:, y * w : (y + 1) * w] = x[:, pl.ds(pl.multiple_of(first, w), w)]


def pack(me, fisher, stored, ny, w):
    n, g = stored.shape[0], fisher.shape[0]
    shapes = [like(g, ny * w)] * 4 + [like(n, ny * w)] * 2 + [like(2, n, ny * w)]
    return call(functools.partial(pack_body, ny, w), shapes, [me, fisher, stored])


def part_body(near1, came, cross):
    cross[0], cross[1] = near1[...], came[1]


def part(near1, came):
    return call(part_body, [like(*came.shape)], [near1, came])[0]


def copies_body(x, out, block, came, sems):
    load = pltpu.make_async_copy(x, block, came)
    load.start()
    load.wait()
    moves = [pltpu.make_async_copy(block, out.at[i], sems.at[i]) for i in range(out.shape[0])]
    for move in moves:
        move.start()
    for move in moves:
        move.wait()


def copies(x, n):
    return pl.pallas_call(
        copies_body,
        out_shape=like(n, *x.shape),
        in_specs=[ANYWHERE],
        out_specs=ANYWHERE,
        scratch_shapes=[pltpu.VMEM(x.shape, BF16), pltpu.SemaphoreType.DMA, pltpu.SemaphoreType.DMA((n,))],
    )(x)


def settle_body(own, came, last, out):
    done = (own[...] + came[0] + last[...]).astype(BF16)
    for i in range(out.shape[0]):
        out[i] = done


def settle(own, came, last, n):
    return call(settle_body, [like(n, *own.shape)], [own, came, last])[0]


def join(held, parts):
    ny, _, w = parts.shape
    for y in range(ny):
        held[:, y * w : (y + 1) * w] = parts[y]


def fold_body(feats, f0, f1, out, out_x, held):
    join(held, feats)
    out_x[...] = lax.dot_general(held[...], f1[...], NT, preferred_element_type=F32)
    out[...] = lax.dot_general(held[...], f0[...], NT, preferred_element_type=F32)


def fold(feats, blocks, after=()):
    ny, q, w = feats.shape
    return call(
        fold_body,
        [like(q, w, dtype=F32)] * 2,
        [feats, *blocks],
        [pltpu.VMEM((q, ny * w), BF16)],
        flops=2 * q * ny * w * 2 * w,
        after=after,
    )


def fold_far_body(feats, f0, f1, out, held):
    fold_body(feats, f0, f1, out.at[0], out.at[1], held)


def fold_far(feats, blocks, after=()):
    ny, q, w = feats.shape
    return call(
        fold_far_body,
        [like(2, q, w, dtype=F32)],
        [feats, *blocks],
        [pltpu.VMEM((q, ny * w), BF16)],
        flops=2 * q * ny * w * 2 * w,
        after=after,
    )[0]


def score_far_body(precond, same, side, cross, twin, out, held):
    join(held, precond)
    for i, rows in enumerate((same, side, cross.at[1], twin.at[1])):
        out[i] = lax.dot_general(rows[...], held[...], NT, preferred_element_type=F32)


def score_far(precond, *blocks):
    ny, q, w = precond.shape
    n, k = blocks[0].shape
    return call(
        score_far_body,
        [like(4, n, q, dtype=F32)],
        [precond, *blocks],
        [pltpu.VMEM((q, k), BF16)],
        flops=2 * q * k * 4 * n,
    )[0]


def score_body(same, side, precond, cross, twin, out, held, rows, sems):
    loads = [pltpu.make_async_copy(block, rows.at[i], sems.at[i]) for i, block in enumerate((same, side))]
    for load in loads:
        load.start()
    join(held, precond)
    for i, block in ((2, cross), (3, twin)):
        out[i] = lax.dot_general(block[0], held[...], NT, preferred_element_type=F32)
    for i, load in enumerate(loads):
        load.wait()
        out[i] = lax.dot_general(rows[i], held[...], NT, preferred_element_type=F32)


def score(precond, same, side, cross, twin):
    ny, q, w = precond.shape
    n, k = side.shape
    return pl.pallas_call(
        score_body,
        out_shape=like(4, n, q, dtype=F32),
        in_specs=[pl.BlockSpec(memory_space=pltpu.HBM)] * 2 + [WHOLE] * 3,
        out_specs=WHOLE,
        scratch_shapes=[pltpu.VMEM((q, k), BF16), pltpu.VMEM((2, n, k), BF16), pltpu.SemaphoreType.DMA((2,))],
        compiler_params=PARAMS,
        cost_estimate=pl.CostEstimate(flops=2 * q * k * 4 * n, bytes_accessed=4 * 1024 * 1024, transcendentals=0),
    )(
        pltpu.with_memory_space_constraint(same, pltpu.HBM),
        pltpu.with_memory_space_constraint(side, pltpu.HBM),
        precond,
        cross,
        twin,
    )


def fetch_body(came, out, sem):
    load = pltpu.make_async_copy(came.at[0], out, sem)
    load.start()
    load.wait()


def fetch(came, after):
    return pl.pallas_call(
        lambda _, *refs: fetch_body(*refs),
        out_shape=like(*came.shape[1:]),
        in_specs=[ANYWHERE, pl.BlockSpec(memory_space=pltpu.HBM)],
        out_specs=WHOLE,
        scratch_shapes=[pltpu.SemaphoreType.DMA],
        compiler_params=PARAMS,
    )(after, pltpu.with_memory_space_constraint(came, pltpu.HBM))


def meet_body(me, own, came, out):
    nz, _, rows, _ = out.shape
    for x in range(2):
        for l in range(2):
            i = (x ^ me[0]) * 2 + (l ^ me[2])
            total = (own[i] + came[i]).astype(BF16)
            for z in range(nz):
                out[z, x * 2 + l] = total[z * rows : (z + 1) * rows]


def meet(me, own, came, nz):
    k, n, q = own.shape
    return call(meet_body, [like(nz, k, n // nz, q)], [me, own, came])[0]


def finish_body(factor, scores, out):
    nz, nx, nl, rows, q = scores.shape
    for l in range(nl):
        total = jnp.zeros((rows, q), F32)
        for x in range(nx):
            for z in range(nz):
                total += scores[z, x, l].astype(F32)
        total = (total * factor).astype(BF16)
        for z in range(nz):
            out[z, :, l * q : (l + 1) * q] = total


def finish(scores, factor):
    nz, _, nl, rows, q = scores.shape
    return call(functools.partial(finish_body, factor), [like(nz, rows, nl * q)], [scores])[0]


def swap(x, *axes):
    sizes = [lax.axis_size(a) for a in axes]
    n = math.prod(sizes)
    return lax.ppermute(x, axes, [(i, n - 1 - i) for i in range(n)])


def trade(x, *axes):
    return lax.all_to_all(x, axes, 0, 0, tiled=True)


def shards(stored, query, fisher):
    ny, nz, nl = lax.axis_size("y"), lax.axis_size("z"), lax.axis_size("xl")
    me = jnp.stack([lax.axis_index(a) for a in ("xh", "core", "xl")]).astype(jnp.int32)
    stored, query, fisher = stored[:, 0], query[:, 0], fisher[0]
    n, f = stored.shape
    q, w = query.shape

    f00, f01, f10, f11, near0, near1, far = pack(me, fisher, stored, ny, w)
    fish = (f00, swap(f10, "xh", "xl")), (swap(f01, "core"), swap(f11, "xh", "core", "xl"))
    came = swap(far, "core")
    cross = part(near1, came)
    side = swap(near0, "xl")

    feats = trade(copies(query, ny), "y")
    total = swap(fold_far(feats, fish[1], (cross, fish[0][1], side)), "core")
    own, own_x = fold(feats, fish[0])
    full = settle(own, total, swap(own_x + total[1], "xh"), ny)
    precond = trade(full, "y")
    twin, cross = swap(cross, "xh", "xl"), swap(cross, "xh")
    far = swap(score_far(precond, fetch(came, full), swap(came[0], "xl"), cross, twin), "core")
    terms = [score(precond, near0, side, cross, twin), far]
    scores = trade(meet(me, *terms, nz).reshape(nz * 2 * nl, n // nz, q), "z", "xh", "xl")
    total = finish(scores.reshape(nz, 2, nl, n // nz, q), 1.0 / math.sqrt(nz * f))
    return trade(total, "z").reshape(n, nl * q).astype(F32)


def solution(mesh):
    dp, layers, queries = mesh.devices.shape
    fine = Mesh(mesh.devices.reshape(2, dp // 4, 2, layers, queries), ("xh", "y", "core", "z", "xl"))
    dp = ("xh", "y", "core")
    placed = (P((*dp, "xl"), "z", None), P("xl", "z", dp), P("z", dp, None))
    return jax.shard_map(
        shards, mesh=fine, in_specs=placed, out_specs=P((*dp, "xl"), None), check_vma=False
    )
```

```python
import functools
import math

import jax
import jax.numpy as jnp
from jax import lax
from jax.experimental import pallas as pl
from jax.experimental.pallas import tpu as pltpu
from jax.sharding import Mesh, PartitionSpec as P

F32 = jnp.float32
BF16 = jnp.bfloat16
NT = (((1,), (1,)), ((), ()))
PARAMS = pltpu.CompilerParams(vmem_limit_bytes=40 * 1024 * 1024)
WHOLE = pl.BlockSpec(memory_space=pltpu.VMEM)
ANYWHERE = pl.BlockSpec(memory_space=pl.ANY)
SCALARS = pl.BlockSpec(memory_space=pltpu.SMEM)


def call(body, out_shape, inputs, scratch=(), flops=0, after=()):
    if after:
        inner, k = body, len(after)
        body = lambda *refs: inner(*refs[k:])
    size = sum(math.prod(x.shape) * x.dtype.itemsize for x in (*inputs, *out_shape))
    return pl.pallas_call(
        body,
        out_shape=[jax.ShapeDtypeStruct(s.shape, s.dtype) for s in out_shape],
        in_specs=[ANYWHERE] * len(after) + [SCALARS if x.dtype == jnp.int32 else WHOLE for x in inputs],
        out_specs=[WHOLE] * len(out_shape),
        scratch_shapes=scratch,
        compiler_params=PARAMS,
        cost_estimate=pl.CostEstimate(flops=flops, bytes_accessed=size, transcendentals=0),
    )(*after, *inputs)


def like(*shape, dtype=BF16):
    return jax.ShapeDtypeStruct(shape, dtype)


def pack_body(ny, w, me, fisher, stored, f00, f01, f10, f11, near0, near1, far):
    for x, outs in ((fisher, ((f00, f10), (f01, f11))), (stored, ((near0, near1), (far.at[0], far.at[1])))):
        for dc in range(2):
            for dx in range(2):
                for y in range(ny):
                    first = (((me[0] ^ dx) * ny + y) * 2 + (me[1] ^ dc)) * w
                    outs[dc][dx][:, y * w : (y + 1) * w] = x[:, pl.ds(pl.multiple_of(first, w), w)]


def pack(me, fisher, stored, ny, w):
    n, g = stored.shape[0], fisher.shape[0]
    shapes = [like(g, ny * w)] * 4 + [like(n, ny * w)] * 2 + [like(2, n, ny * w)]
    return call(functools.partial(pack_body, ny, w), shapes, [me, fisher, stored])


def part_body(near1, came, cross):
    cross[0], cross[1] = near1[...], came[1]


def part(near1, came):
    return call(part_body, [like(*came.shape)], [near1, came])[0]


def copies_body(x, out, block, came, sems):
    load = pltpu.make_async_copy(x, block, came)
    load.start()
    load.wait()
    moves = [pltpu.make_async_copy(block, out.at[i], sems.at[i]) for i in range(out.shape[0])]
    for move in moves:
        move.start()
    for move in moves:
        move.wait()


def copies(x, n):
    return pl.pallas_call(
        copies_body,
        out_shape=like(n, *x.shape),
        in_specs=[ANYWHERE],
        out_specs=ANYWHERE,
        scratch_shapes=[pltpu.VMEM(x.shape, BF16), pltpu.SemaphoreType.DMA, pltpu.SemaphoreType.DMA((n,))],
    )(x)


def settle_body(own, came, last, out):
    done = (own[...] + came[0] + last[...]).astype(BF16)
    for i in range(out.shape[0]):
        out[i] = done


def settle(own, came, last, n):
    return call(settle_body, [like(n, *own.shape)], [own, came, last])[0]


def join(held, parts):
    ny, _, w = parts.shape
    for y in range(ny):
        held[:, y * w : (y + 1) * w] = parts[y]


def fold_body(feats, f0, f1, out, out_x, held):
    join(held, feats)
    out_x[...] = lax.dot_general(held[...], f1[...], NT, preferred_element_type=F32)
    out[...] = lax.dot_general(held[...], f0[...], NT, preferred_element_type=F32)


def fold(feats, blocks, after=()):
    ny, q, w = feats.shape
    return call(
        fold_body,
        [like(q, w, dtype=F32)] * 2,
        [feats, *blocks],
        [pltpu.VMEM((q, ny * w), BF16)],
        flops=2 * q * ny * w * 2 * w,
        after=after,
    )


def fold_far_body(feats, f0, f1, out, held):
    fold_body(feats, f0, f1, out.at[0], out.at[1], held)


def fold_far(feats, blocks, after=()):
    ny, q, w = feats.shape
    return call(
        fold_far_body,
        [like(2, q, w, dtype=F32)],
        [feats, *blocks],
        [pltpu.VMEM((q, ny * w), BF16)],
        flops=2 * q * ny * w * 2 * w,
        after=after,
    )[0]


def score_far_body(precond, same, side, cross, twin, out, held):
    join(held, precond)
    for i, rows in enumerate((same, side, cross.at[1], twin.at[1])):
        out[i] = lax.dot_general(rows[...], held[...], NT, preferred_element_type=F32)


def score_far(precond, *blocks):
    ny, q, w = precond.shape
    n, k = blocks[0].shape
    return call(
        score_far_body,
        [like(4, n, q, dtype=F32)],
        [precond, *blocks],
        [pltpu.VMEM((q, k), BF16)],
        flops=2 * q * k * 4 * n,
    )[0]


def score_body(same, side, precond, cross, twin, out, held, rows, sems):
    loads = [pltpu.make_async_copy(block, rows.at[i], sems.at[i]) for i, block in enumerate((same, side))]
    for load in loads:
        load.start()
    join(held, precond)
    for i, block in ((2, cross), (3, twin)):
        out[i] = lax.dot_general(block[0], held[...], NT, preferred_element_type=F32)
    for i, load in enumerate(loads):
        load.wait()
        out[i] = lax.dot_general(rows[i], held[...], NT, preferred_element_type=F32)


def score(precond, same, side, cross, twin):
    ny, q, w = precond.shape
    n, k = side.shape
    return pl.pallas_call(
        score_body,
        out_shape=like(4, n, q, dtype=F32),
        in_specs=[pl.BlockSpec(memory_space=pltpu.HBM)] * 2 + [WHOLE] * 3,
        out_specs=WHOLE,
        scratch_shapes=[pltpu.VMEM((q, k), BF16), pltpu.VMEM((2, n, k), BF16), pltpu.SemaphoreType.DMA((2,))],
        compiler_params=PARAMS,
        cost_estimate=pl.CostEstimate(flops=2 * q * k * 4 * n, bytes_accessed=4 * 1024 * 1024, transcendentals=0),
    )(
        pltpu.with_memory_space_constraint(same, pltpu.HBM),
        pltpu.with_memory_space_constraint(side, pltpu.HBM),
        precond,
        cross,
        twin,
    )


def fetch_body(came, out, sem):
    load = pltpu.make_async_copy(came.at[0], out, sem)
    load.start()
    load.wait()


def fetch(came, after):
    return pl.pallas_call(
        lambda _, *refs: fetch_body(*refs),
        out_shape=like(*came.shape[1:]),
        in_specs=[ANYWHERE, pl.BlockSpec(memory_space=pltpu.HBM)],
        out_specs=WHOLE,
        scratch_shapes=[pltpu.SemaphoreType.DMA],
        compiler_params=PARAMS,
    )(after, pltpu.with_memory_space_constraint(came, pltpu.HBM))


def meet_body(me, own, came, out):
    nz, _, rows, _ = out.shape
    for x in range(2):
        for l in range(2):
            i = (x ^ me[0]) * 2 + (l ^ me[2])
            total = (own[i] + came[i]).astype(BF16)
            for z in range(nz):
                out[z, x * 2 + l] = total[z * rows : (z + 1) * rows]


def meet(me, own, came, nz):
    k, n, q = own.shape
    return call(meet_body, [like(nz, k, n // nz, q)], [me, own, came])[0]


def finish_body(factor, scores, out):
    nz, nx, nl, rows, q = scores.shape
    for l in range(nl):
        total = jnp.zeros((rows, q), F32)
        for x in range(nx):
            for z in range(nz):
                total += scores[z, x, l].astype(F32)
        total = (total * factor).astype(BF16)
        for z in range(nz):
            out[z, :, l * q : (l + 1) * q] = total


def finish(scores, factor):
    nz, _, nl, rows, q = scores.shape
    return call(functools.partial(finish_body, factor), [like(nz, rows, nl * q)], [scores])[0]


def swap(x, *axes):
    sizes = [lax.axis_size(a) for a in axes]
    n = math.prod(sizes)
    return lax.ppermute(x, axes, [(i, n - 1 - i) for i in range(n)])


def trade(x, *axes, groups=None):
    return lax.all_to_all(x, axes, 0, 0, axis_index_groups=groups, tiled=True)


def shards(stored, query, fisher):
    ny, nz, nl = lax.axis_size("y"), lax.axis_size("z"), lax.axis_size("xl")
    me = jnp.stack([lax.axis_index(a) for a in ("xh", "core", "xl")]).astype(jnp.int32)
    stored, query, fisher = stored[:, 0], query[:, 0], fisher[0]
    n, f = stored.shape
    q, w = query.shape

    f00, f01, f10, f11, near0, near1, far = pack(me, fisher, stored, ny, w)
    fish = (f00, swap(f10, "xh", "xl")), (swap(f01, "core"), swap(f11, "xh", "core", "xl"))
    came = swap(far, "core")
    cross = part(near1, came)
    side = swap(near0, "xl")

    feats = trade(copies(query, ny), "y")
    total = swap(fold_far(feats, fish[1], (cross, fish[0][1], side)), "core")
    own, own_x = fold(feats, fish[0])
    full = settle(own, total, swap(own_x + total[1], "xh"), ny)
    precond = trade(full, "y")
    twin, cross = swap(cross, "xh", "xl"), swap(cross, "xh")
    far = swap(score_far(precond, fetch(came, full), swap(came[0], "xl"), cross, twin), "core")
    terms = [score(precond, near0, side, cross, twin), far]
    last_first = [[z * 2 * nl + x for z in reversed(range(nz)) for x in range(2 * nl)]]
    scores = trade(meet(me, *terms, nz).reshape(nz * 2 * nl, n // nz, q), "z", "xh", "xl", groups=last_first)
    total = finish(scores.reshape(nz, 2, nl, n // nz, q), 1.0 / math.sqrt(nz * f))
    return trade(total, "z", groups=[list(reversed(range(nz)))]).reshape(n, nl * q).astype(F32)


def solution(mesh):
    dp, layers, queries = mesh.devices.shape
    fine = Mesh(mesh.devices.reshape(2, dp // 4, 2, layers, queries), ("xh", "y", "core", "z", "xl"))
    dp = ("xh", "y", "core")
    placed = (P((*dp, "xl"), "z", None), P("xl", "z", dp), P("z", dp, None))
    return jax.shard_map(
        shards, mesh=fine, in_specs=placed, out_specs=P((*dp, "xl"), None), check_vma=False
    )
```

```python
import functools
import math

import jax
import jax.numpy as jnp
from jax import lax
from jax.experimental import pallas as pl
from jax.experimental.pallas import tpu as pltpu
from jax.sharding import Mesh, PartitionSpec as P

F32 = jnp.float32
BF16 = jnp.bfloat16
NT = (((1,), (1,)), ((), ()))
PARAMS = pltpu.CompilerParams(vmem_limit_bytes=40 * 1024 * 1024)
WHOLE = pl.BlockSpec(memory_space=pltpu.VMEM)
ANYWHERE = pl.BlockSpec(memory_space=pl.ANY)
SCALARS = pl.BlockSpec(memory_space=pltpu.SMEM)


def call(body, out_shape, inputs, scratch=(), flops=0, after=()):
    if after:
        inner, k = body, len(after)
        body = lambda *refs: inner(*refs[k:])
    size = sum(math.prod(x.shape) * x.dtype.itemsize for x in (*inputs, *out_shape))
    return pl.pallas_call(
        body,
        out_shape=[jax.ShapeDtypeStruct(s.shape, s.dtype) for s in out_shape],
        in_specs=[ANYWHERE] * len(after) + [SCALARS if x.dtype == jnp.int32 else WHOLE for x in inputs],
        out_specs=[WHOLE] * len(out_shape),
        scratch_shapes=scratch,
        compiler_params=PARAMS,
        cost_estimate=pl.CostEstimate(flops=flops, bytes_accessed=size, transcendentals=0),
    )(*after, *inputs)


def like(*shape, dtype=BF16):
    return jax.ShapeDtypeStruct(shape, dtype)


def across(n):
    return [i // 2 + (i % 2) * (n // 2) for i in range(n)]


def pack_body(ny, w, me, fisher, stored, f00, f01, f10, f11, near0, near1, far):
    for x, outs in ((fisher, ((f00, f10), (f01, f11))), (stored, ((near0, near1), (far.at[0], far.at[1])))):
        for dc in range(2):
            for dx in range(2):
                for i, y in enumerate(across(ny)):
                    first = (((me[0] ^ dx) * ny + y) * 2 + (me[1] ^ dc)) * w
                    outs[dc][dx][:, i * w : (i + 1) * w] = x[:, pl.ds(pl.multiple_of(first, w), w)]


def pack(me, fisher, stored, ny, w):
    n, g = stored.shape[0], fisher.shape[0]
    shapes = [like(g, ny * w)] * 4 + [like(n, ny * w)] * 2 + [like(2, n, ny * w)]
    return call(functools.partial(pack_body, ny, w), shapes, [me, fisher, stored])


def part_body(near1, came, cross):
    cross[0], cross[1] = near1[...], came[1]


def part(near1, came):
    return call(part_body, [like(*came.shape)], [near1, came])[0]


def copies_body(x, out, block, came, sems):
    load = pltpu.make_async_copy(x, block, came)
    load.start()
    load.wait()
    moves = [pltpu.make_async_copy(block, out.at[i], sems.at[i]) for i in range(out.shape[0])]
    for move in moves:
        move.start()
    for move in moves:
        move.wait()


def copies(x, n):
    return pl.pallas_call(
        copies_body,
        out_shape=like(n, *x.shape),
        in_specs=[ANYWHERE],
        out_specs=ANYWHERE,
        scratch_shapes=[pltpu.VMEM(x.shape, BF16), pltpu.SemaphoreType.DMA, pltpu.SemaphoreType.DMA((n,))],
    )(x)


def settle_body(own, came, last, out):
    done = (own[...] + came[0] + last[...]).astype(BF16)
    for i in range(out.shape[0]):
        out[i] = done


def settle(own, came, last, n):
    return call(settle_body, [like(n, *own.shape)], [own, came, last])[0]


def join(held, parts):
    ny, _, w = parts.shape
    for y in range(ny):
        held[:, y * w : (y + 1) * w] = parts[y]


def fold_body(feats, f0, f1, out, out_x, held):
    join(held, feats)
    out_x[...] = lax.dot_general(held[...], f1[...], NT, preferred_element_type=F32)
    out[...] = lax.dot_general(held[...], f0[...], NT, preferred_element_type=F32)


def fold(feats, blocks, after=()):
    ny, q, w = feats.shape
    return call(
        fold_body,
        [like(q, w, dtype=F32)] * 2,
        [feats, *blocks],
        [pltpu.VMEM((q, ny * w), BF16)],
        flops=2 * q * ny * w * 2 * w,
        after=after,
    )


def fold_far_body(feats, f0, f1, out, held):
    fold_body(feats, f0, f1, out.at[0], out.at[1], held)


def fold_far(feats, blocks, after=()):
    ny, q, w = feats.shape
    return call(
        fold_far_body,
        [like(2, q, w, dtype=F32)],
        [feats, *blocks],
        [pltpu.VMEM((q, ny * w), BF16)],
        flops=2 * q * ny * w * 2 * w,
        after=after,
    )[0]


def score_far_body(precond, same, side, cross, twin, out, held):
    join(held, precond)
    for i, rows in enumerate((same, side, cross.at[1], twin.at[1])):
        out[i] = lax.dot_general(rows[...], held[...], NT, preferred_element_type=F32)


def score_far(precond, *blocks):
    ny, q, w = precond.shape
    n, k = blocks[0].shape
    return call(
        score_far_body,
        [like(4, n, q, dtype=F32)],
        [precond, *blocks],
        [pltpu.VMEM((q, k), BF16)],
        flops=2 * q * k * 4 * n,
    )[0]


def score_body(same, side, precond, cross, twin, out, held, rows, sems):
    loads = [pltpu.make_async_copy(block, rows.at[i], sems.at[i]) for i, block in enumerate((same, side))]
    for load in loads:
        load.start()
    join(held, precond)
    for i, block in ((2, cross), (3, twin)):
        out[i] = lax.dot_general(block[0], held[...], NT, preferred_element_type=F32)
    for i, load in enumerate(loads):
        load.wait()
        out[i] = lax.dot_general(rows[i], held[...], NT, preferred_element_type=F32)


def score(precond, same, side, cross, twin):
    ny, q, w = precond.shape
    n, k = side.shape
    return pl.pallas_call(
        score_body,
        out_shape=like(4, n, q, dtype=F32),
        in_specs=[pl.BlockSpec(memory_space=pltpu.HBM)] * 2 + [WHOLE] * 3,
        out_specs=WHOLE,
        scratch_shapes=[pltpu.VMEM((q, k), BF16), pltpu.VMEM((2, n, k), BF16), pltpu.SemaphoreType.DMA((2,))],
        compiler_params=PARAMS,
        cost_estimate=pl.CostEstimate(flops=2 * q * k * 4 * n, bytes_accessed=4 * 1024 * 1024, transcendentals=0),
    )(
        pltpu.with_memory_space_constraint(same, pltpu.HBM),
        pltpu.with_memory_space_constraint(side, pltpu.HBM),
        precond,
        cross,
        twin,
    )


def fetch_body(came, out, sem):
    load = pltpu.make_async_copy(came.at[0], out, sem)
    load.start()
    load.wait()


def fetch(came, after):
    return pl.pallas_call(
        lambda _, *refs: fetch_body(*refs),
        out_shape=like(*came.shape[1:]),
        in_specs=[ANYWHERE, pl.BlockSpec(memory_space=pltpu.HBM)],
        out_specs=WHOLE,
        scratch_shapes=[pltpu.SemaphoreType.DMA],
        compiler_params=PARAMS,
    )(after, pltpu.with_memory_space_constraint(came, pltpu.HBM))


def meet_body(me, own, came, out):
    nz, _, rows, _ = out.shape
    for x in range(2):
        for l in range(2):
            i = (x ^ me[0]) * 2 + (l ^ me[2])
            total = (own[i] + came[i]).astype(BF16)
            for z in range(nz):
                out[z, x * 2 + l] = total[z * rows : (z + 1) * rows]


def meet(me, own, came, nz):
    k, n, q = own.shape
    return call(meet_body, [like(nz, k, n // nz, q)], [me, own, came])[0]


def finish_body(factor, scores, out):
    nz, nx, nl, rows, q = scores.shape
    for l in range(nl):
        total = jnp.zeros((rows, q), F32)
        for x in range(nx):
            for z in range(nz):
                total += scores[z, x, l].astype(F32)
        total = (total * factor).astype(BF16)
        for z in range(nz):
            out[z, :, l * q : (l + 1) * q] = total


def finish(scores, factor):
    nz, _, nl, rows, q = scores.shape
    return call(functools.partial(finish_body, factor), [like(nz, rows, nl * q)], [scores])[0]


def swap(x, *axes):
    sizes = [lax.axis_size(a) for a in axes]
    n = math.prod(sizes)
    return lax.ppermute(x, axes, [(i, n - 1 - i) for i in range(n)])


def trade(x, *axes, groups=None):
    return lax.all_to_all(x, axes, 0, 0, axis_index_groups=groups, tiled=True)


def shards(stored, query, fisher):
    ny, nz, nl = lax.axis_size("y"), lax.axis_size("z"), lax.axis_size("xl")
    me = jnp.stack([lax.axis_index(a) for a in ("xh", "core", "xl")]).astype(jnp.int32)
    stored, query, fisher = stored[:, 0], query[:, 0], fisher[0]
    n, f = stored.shape
    q, w = query.shape

    f00, f01, f10, f11, near0, near1, far = pack(me, fisher, stored, ny, w)
    fish = (f00, swap(f10, "xh", "xl")), (swap(f01, "core"), swap(f11, "xh", "core", "xl"))
    came = swap(far, "core")
    cross = part(near1, came)
    side = swap(near0, "xl")

    feats = trade(copies(query, ny), "y", groups=[across(ny)])
    total = swap(fold_far(feats, fish[1], (cross, fish[0][1], side)), "core")
    own, own_x = fold(feats, fish[0])
    full = settle(own, total, swap(own_x + total[1], "xh"), ny)
    precond = trade(full, "y", groups=[across(ny)])
    twin, cross = swap(cross, "xh", "xl"), swap(cross, "xh")
    far = swap(score_far(precond, fetch(came, full), swap(came[0], "xl"), cross, twin), "core")
    terms = [score(precond, near0, side, cross, twin), far]
    last_first = [[z * 2 * nl + x for z in reversed(range(nz)) for x in range(2 * nl)]]
    scores = trade(meet(me, *terms, nz).reshape(nz * 2 * nl, n // nz, q), "z", "xh", "xl", groups=last_first)
    total = finish(scores.reshape(nz, 2, nl, n // nz, q), 1.0 / math.sqrt(nz * f))
    return trade(total, "z", groups=[list(reversed(range(nz)))]).reshape(n, nl * q).astype(F32)


def solution(mesh):
    dp, layers, queries = mesh.devices.shape
    fine = Mesh(mesh.devices.reshape(2, dp // 4, 2, layers, queries), ("xh", "y", "core", "z", "xl"))
    dp = ("xh", "y", "core")
    placed = (P((*dp, "xl"), "z", None), P("xl", "z", dp), P("z", dp, None))
    return jax.shard_map(
        shards, mesh=fine, in_specs=placed, out_specs=P((*dp, "xl"), None), check_vma=False
    )
```

```python
import functools
import math

import jax
import jax.numpy as jnp
from jax import lax
from jax.experimental import pallas as pl
from jax.experimental.pallas import tpu as pltpu
from jax.sharding import Mesh, PartitionSpec as P

F32 = jnp.float32
BF16 = jnp.bfloat16
NT = (((1,), (1,)), ((), ()))
PARAMS = pltpu.CompilerParams(vmem_limit_bytes=40 * 1024 * 1024)
WHOLE = pl.BlockSpec(memory_space=pltpu.VMEM)
ANYWHERE = pl.BlockSpec(memory_space=pl.ANY)
SCALARS = pl.BlockSpec(memory_space=pltpu.SMEM)


def call(body, out_shape, inputs, scratch=(), flops=0, after=()):
    if after:
        inner, k = body, len(after)
        body = lambda *refs: inner(*refs[k:])
    size = sum(math.prod(x.shape) * x.dtype.itemsize for x in (*inputs, *out_shape))
    return pl.pallas_call(
        body,
        out_shape=[jax.ShapeDtypeStruct(s.shape, s.dtype) for s in out_shape],
        in_specs=[ANYWHERE] * len(after) + [SCALARS if x.dtype == jnp.int32 else WHOLE for x in inputs],
        out_specs=[WHOLE] * len(out_shape),
        scratch_shapes=scratch,
        compiler_params=PARAMS,
        cost_estimate=pl.CostEstimate(flops=flops, bytes_accessed=size, transcendentals=0),
    )(*after, *inputs)


def like(*shape, dtype=BF16):
    return jax.ShapeDtypeStruct(shape, dtype)


def across(n):
    return [i // 2 + (i % 2) * (n // 2) for i in range(n)]


def pack_body(ny, w, me, fisher, stored, f00, f01, f10, f11, near0, near1, far):
    for x, outs in ((fisher, ((f00, f10), (f01, f11))), (stored, ((near0, near1), (far.at[0], far.at[1])))):
        for dc in range(2):
            for dx in range(2):
                for i, y in enumerate(across(ny)):
                    first = (((me[0] ^ dx) * ny + y) * 2 + (me[1] ^ dc)) * w
                    outs[dc][dx][:, i * w : (i + 1) * w] = x[:, pl.ds(pl.multiple_of(first, w), w)]


def pack(me, fisher, stored, ny, w):
    n, g = stored.shape[0], fisher.shape[0]
    shapes = [like(g, ny * w)] * 4 + [like(n, ny * w)] * 2 + [like(2, n, ny * w)]
    return call(functools.partial(pack_body, ny, w), shapes, [me, fisher, stored])


def part_body(near1, came, cross):
    cross[0], cross[1] = near1[...], came[1]


def part(near1, came):
    return call(part_body, [like(*came.shape)], [near1, came])[0]


def copies_body(x, out, block, came, sems):
    load = pltpu.make_async_copy(x, block, came)
    load.start()
    load.wait()
    moves = [pltpu.make_async_copy(block, out.at[i], sems.at[i]) for i in range(out.shape[0])]
    for move in moves:
        move.start()
    for move in moves:
        move.wait()


def copies(x, n):
    return pl.pallas_call(
        copies_body,
        out_shape=like(n, *x.shape),
        in_specs=[ANYWHERE],
        out_specs=ANYWHERE,
        scratch_shapes=[pltpu.VMEM(x.shape, BF16), pltpu.SemaphoreType.DMA, pltpu.SemaphoreType.DMA((n,))],
    )(x)


def settle_body(own, came, last, out):
    done = (own[...] + came[0] + last[...]).astype(BF16)
    for i in range(out.shape[0]):
        out[i] = done


def settle(own, came, last, n):
    return call(settle_body, [like(n, *own.shape)], [own, came, last])[0]


def join(held, parts):
    ny, _, w = parts.shape
    for y in range(ny):
        held[:, y * w : (y + 1) * w] = parts[y]


def fold_body(feats, f0, f1, out, out_x, held):
    join(held, feats)
    out_x[...] = lax.dot_general(held[...], f1[...], NT, preferred_element_type=F32)
    out[...] = lax.dot_general(held[...], f0[...], NT, preferred_element_type=F32)


def fold(feats, blocks, after=()):
    ny, q, w = feats.shape
    return call(
        fold_body,
        [like(q, w, dtype=F32)] * 2,
        [feats, *blocks],
        [pltpu.VMEM((q, ny * w), BF16)],
        flops=2 * q * ny * w * 2 * w,
        after=after,
    )


def fold_far_body(feats, f0, f1, out, held):
    fold_body(feats, f0, f1, out.at[0], out.at[1], held)


def fold_far(feats, blocks, after=()):
    ny, q, w = feats.shape
    return call(
        fold_far_body,
        [like(2, q, w, dtype=F32)],
        [feats, *blocks],
        [pltpu.VMEM((q, ny * w), BF16)],
        flops=2 * q * ny * w * 2 * w,
        after=after,
    )[0]


def score_far_body(precond, same, side, cross, twin, out, held):
    join(held, precond)
    for i, rows in enumerate((same, side, cross.at[1], twin.at[1])):
        out[i] = lax.dot_general(rows[...], held[...], NT, preferred_element_type=F32)


def score_far(precond, *blocks):
    ny, q, w = precond.shape
    n, k = blocks[0].shape
    return call(
        score_far_body,
        [like(4, n, q, dtype=F32)],
        [precond, *blocks],
        [pltpu.VMEM((q, k), BF16)],
        flops=2 * q * k * 4 * n,
    )[0]


def score_body(same, side, precond, cross, twin, out, held, rows, sems):
    loads = [pltpu.make_async_copy(block, rows.at[i], sems.at[i]) for i, block in enumerate((same, side))]
    for load in loads:
        load.start()
    join(held, precond)
    for i, block in ((2, cross), (3, twin)):
        out[i] = lax.dot_general(block[0], held[...], NT, preferred_element_type=F32)
    for i, load in enumerate(loads):
        load.wait()
        out[i] = lax.dot_general(rows[i], held[...], NT, preferred_element_type=F32)


def score(precond, same, side, cross, twin):
    ny, q, w = precond.shape
    n, k = side.shape
    return pl.pallas_call(
        score_body,
        out_shape=like(4, n, q, dtype=F32),
        in_specs=[pl.BlockSpec(memory_space=pltpu.HBM)] * 2 + [WHOLE] * 3,
        out_specs=WHOLE,
        scratch_shapes=[pltpu.VMEM((q, k), BF16), pltpu.VMEM((2, n, k), BF16), pltpu.SemaphoreType.DMA((2,))],
        compiler_params=PARAMS,
        cost_estimate=pl.CostEstimate(flops=2 * q * k * 4 * n, bytes_accessed=4 * 1024 * 1024, transcendentals=0),
    )(
        pltpu.with_memory_space_constraint(same, pltpu.HBM),
        pltpu.with_memory_space_constraint(side, pltpu.HBM),
        precond,
        cross,
        twin,
    )


def fetch_body(came, out, sem):
    load = pltpu.make_async_copy(came.at[0], out, sem)
    load.start()
    load.wait()


def fetch(came, after):
    return pl.pallas_call(
        lambda _, *refs: fetch_body(*refs),
        out_shape=like(*came.shape[1:]),
        in_specs=[ANYWHERE, pl.BlockSpec(memory_space=pltpu.HBM)],
        out_specs=WHOLE,
        scratch_shapes=[pltpu.SemaphoreType.DMA],
        compiler_params=PARAMS,
    )(after, pltpu.with_memory_space_constraint(came, pltpu.HBM))


def meet_body(me, own, came, out):
    nz, _, rows, _ = out.shape
    for x in range(2):
        for l in range(2):
            i = (x ^ me[0]) * 2 + (l ^ me[2])
            total = (own[i] + came[i]).astype(BF16)
            for z in range(nz):
                out[z, x * 2 + l] = total[z * rows : (z + 1) * rows]


def meet(me, own, came, nz):
    k, n, q = own.shape
    return call(meet_body, [like(nz, k, n // nz, q)], [me, own, came])[0]


def finish_body(factor, scores, out):
    nz, nx, nl, rows, q = scores.shape
    for l in range(nl):
        total = jnp.zeros((rows, q), F32)
        for x in range(nx):
            for z in range(nz):
                total += scores[z, x, l].astype(F32)
        total = (total * factor).astype(BF16)
        for z in range(nz):
            out[z, :, l * q : (l + 1) * q] = total


def finish(scores, factor):
    nz, _, nl, rows, q = scores.shape
    return call(functools.partial(finish_body, factor), [like(nz, rows, nl * q)], [scores])[0]


def swap(x, *axes):
    sizes = [lax.axis_size(a) for a in axes]
    n = math.prod(sizes)
    return lax.ppermute(x, axes, [(i, n - 1 - i) for i in range(n)])


def trade(x, *axes, groups=None):
    return lax.all_to_all(x, axes, 0, 0, axis_index_groups=groups, tiled=True)


def shards(stored, query, fisher):
    ny, nz, nl = lax.axis_size("y"), lax.axis_size("z"), lax.axis_size("xl")
    me = jnp.stack([lax.axis_index(a) for a in ("xh", "core", "xl")]).astype(jnp.int32)
    stored, query, fisher = stored[:, 0], query[:, 0], fisher[0]
    n, f = stored.shape
    q, w = query.shape

    f00, f01, f10, f11, near0, near1, far = pack(me, fisher, stored, ny, w)
    fish = (f00, swap(f10, "xh", "xl")), (swap(f01, "core"), swap(f11, "xh", "core", "xl"))
    came = swap(far, "core")
    cross = part(near1, came)
    side = swap(near0, "xl")

    feats = trade(copies(query, ny), "y", groups=[across(ny)])
    total = swap(fold_far(feats, fish[1], (cross, fish[0][1], side)), "core")
    own, own_x = fold(feats, fish[0])
    full = settle(own, total, swap(own_x + total[1], "xh"), ny)
    precond = trade(full, "y", groups=[across(ny)])
    twin, cross = swap(cross, "xh", "xl"), swap(cross, "xh")
    far = swap(score_far(precond, fetch(came, full), swap(came[0], "xl"), cross, twin), "core")
    terms = [score(precond, near0, side, cross, twin), far]
    last_first = [[z * 2 * nl + x for z in [nz - 1 - i // 2 if i % 2 == 0 else i // 2 for i in range(nz)] for x in range(2 * nl)]]
    scores = trade(meet(me, *terms, nz).reshape(nz * 2 * nl, n // nz, q), "z", "xh", "xl", groups=last_first)
    total = finish(scores.reshape(nz, 2, nl, n // nz, q), 1.0 / math.sqrt(nz * f))
    return trade(total, "z", groups=[[nz - 1 - i // 2 if i % 2 == 0 else i // 2 for i in range(nz)]]).reshape(n, nl * q).astype(F32)


def solution(mesh):
    dp, layers, queries = mesh.devices.shape
    fine = Mesh(mesh.devices.reshape(2, dp // 4, 2, layers, queries), ("xh", "y", "core", "z", "xl"))
    dp = ("xh", "y", "core")
    placed = (P((*dp, "xl"), "z", None), P("xl", "z", dp), P("z", dp, None))
    return jax.shard_map(
        shards, mesh=fine, in_specs=placed, out_specs=P((*dp, "xl"), None), check_vma=False
    )
```
